32 devices in a mesh: blk: 8 (over y, x, core), head: 4 (over z).
Axes of the slice: x: 2, y: 2, z: 4, core: 2. Of those that a mesh axis runs over, the one named last changes fastest.
Arguments:
- query_vectors: bfloat16 [1024, 2560], P('blk', 'head'), may hold values from -8 to 8
- key_vectors: bfloat16 [1024, 2560], P('blk', 'head'), may hold values from -8 to 8, as said below
- value_vectors: bfloat16 [1024, 2560], P('blk', 'head'), may hold values from -6 to 6
- tangent_queries: bfloat16 [1024, 2560], P('blk', 'head'), may hold values from -6 to 6
- tangent_keys: bfloat16 [1024, 2560], P('blk', 'head'), may hold values from -6 to 6
- tangent_values: bfloat16 [1024, 2560], P('blk', 'head'), may hold values from -6 to 6
- target_gap: bfloat16 [1024, 2560], P(('blk', 'head')), may hold values from -6 to 6
Outputs:
- primal_out: bfloat16 [1024, 2560], P(('blk', 'head'))
- tangent_out: bfloat16 [1024, 2560], P(('blk', 'head'))
- query_grad: bfloat16 [1024, 2560], P('blk', 'head')
- key_grad: bfloat16 [1024, 2560], P('blk', 'head')
- value_grad: bfloat16 [1024, 2560], P('blk', 'head')
The draws below stay inside these ranges and needn't reach their ends.
Inputs may be any that keep to these rules, and one draw needn't show every extreme that they name: `key_vectors`: keys are real-valued draws.
All inputs are finite; a program needn't handle non-finite values.
Results may differ from the reference program's by a relative error of at most 0.015.
Values may be sent and summed in bfloat16 or wider, within the bound.
A program may use at most 128 MiB of HBM per device.

```python
import math
import jax
import jax.numpy as jnp
from jax import lax

HEADS = 20
HD = 128
FEAT = 2560
SEQ = 1024


def paired_fields(key):
    base_queries = jax.random.fold_in(key, 11)
    base_keys = jax.random.fold_in(key, 12)
    queries_drawn = jnp.clip(jax.random.normal(base_queries, (SEQ, FEAT), jnp.float32) * 1.4, -8.0, 8.0)
    keys_drawn = jnp.clip(jax.random.normal(base_keys, (SEQ, FEAT), jnp.float32) * 1.4, -8.0, 8.0)
    return (queries_drawn, keys_drawn)


def draw_query_vectors(key, part):
    return paired_fields(key)[0].astype(jnp.bfloat16)


def draw_key_vectors(key, part):
    return paired_fields(key)[1].astype(jnp.bfloat16)


def block_levels(own_key, dims, pieces, low, high):
    factor_of, own = 1.0, jax.random.fold_in(own_key, 6)
    for axis_at, blocks in pieces:
        draws = jnp.exp(jax.random.uniform(jax.random.fold_in(own, axis_at), (blocks,), jnp.float32, low / len(pieces), high / len(pieces)))
        factor_of = factor_of * jnp.repeat(draws, dims[axis_at] // blocks).reshape([-1 if axis == axis_at else 1 for axis in range(len(dims))])
    return factor_of


def scatter_about(own_key, dims, deviation, most, split=(), held_as=jnp.bfloat16):
    array = jax.random.normal(own_key, dims, jnp.float32) * deviation
    if len(split) > 0:
        array = block_levels(own_key, dims, split, -0.22, 0.18) * array
    return jnp.clip(array, min=-most, max=most).astype(held_as)


def setup_inputs(seed: int = 0) -> dict:
    splits = jax.random.split(jax.random.key(seed), 8)
    query_vectors = draw_query_vectors(jax.random.fold_in(splits[7], 71), 0)
    key_vectors = draw_key_vectors(jax.random.fold_in(splits[7], 71), 0)
    value_vectors = scatter_about(splits[2], (SEQ, FEAT), 1.0, 6.0, ((0, 8), (1, 4)))
    tangent_queries = scatter_about(splits[3], (SEQ, FEAT), 1.0, 6.0, ((0, 8), (1, 4)))
    tangent_keys = scatter_about(splits[4], (SEQ, FEAT), 1.0, 6.0, ((0, 8), (1, 4)))
    tangent_values = scatter_about(splits[5], (SEQ, FEAT), 1.0, 6.0, ((0, 8), (1, 4)))
    target_gap = scatter_about(splits[6], (SEQ, FEAT), 1.0, 6.0, ((0, 32),))
    return {"query_vectors": query_vectors, "key_vectors": key_vectors, "value_vectors": value_vectors, "tangent_queries": tangent_queries, "tangent_keys": tangent_keys, "tangent_values": tangent_values, "target_gap": target_gap}


scale_loss = 64.0

def heads_first(matrix):
    return matrix.reshape(SEQ, HEADS, HD).transpose(1, 0, 2)

def heads_last(matrix):
    return matrix.transpose(1, 0, 2).reshape(SEQ, HEADS * HD)

def one_head(operands):
    q_head, k_head, v_head, tq_head, tk_head, tv_head, gap_head = operands
    inverse = 1.0 / math.sqrt(HD)
    scores = jnp.dot(q_head, k_head.T, preferred_element_type=jnp.float32) * inverse
    tan_scores = (jnp.dot(tq_head, k_head.T, preferred_element_type=jnp.float32) + jnp.dot(q_head, tk_head.T, preferred_element_type=jnp.float32)) * inverse
    row_peak = lax.optimization_barrier(jnp.max(scores, axis=1, keepdims=True))
    weights = jnp.exp(scores - row_peak)
    denominator = lax.optimization_barrier(jnp.sum(weights, axis=1, keepdims=True))
    weighted_tan = weights * tan_scores
    tan_weight = lax.optimization_barrier(jnp.sum(weighted_tan, axis=1, keepdims=True))
    weights_low = weights.astype(jnp.bfloat16)
    tan_low = weighted_tan.astype(jnp.bfloat16)
    primal = jnp.dot(weights_low, v_head, preferred_element_type=jnp.float32) / denominator
    tangent = (jnp.dot(tan_low, v_head, preferred_element_type=jnp.float32) + jnp.dot(weights_low, tv_head, preferred_element_type=jnp.float32)) / denominator
    tangent = tangent - tan_weight / denominator * primal
    primal_low = primal.astype(jnp.bfloat16)
    tangent_low = tangent.astype(jnp.bfloat16)
    cotangent = (scale_loss * (gap_head.astype(jnp.float32) + tangent_low.astype(jnp.float32))).astype(jnp.bfloat16)
    log_total = row_peak + jnp.log(denominator)
    chances = jnp.exp(scores - log_total)
    inner_sums = lax.optimization_barrier(jnp.sum(cotangent.astype(jnp.float32) * primal_low.astype(jnp.float32), axis=1, keepdims=True))
    value_grad = jnp.dot(chances.astype(jnp.bfloat16).T, cotangent, preferred_element_type=jnp.float32)
    prob_grad = jnp.dot(cotangent, v_head.T, preferred_element_type=jnp.float32)
    score_grad = (chances * (prob_grad - inner_sums)).astype(jnp.bfloat16)
    query_grad = jnp.dot(score_grad, k_head, preferred_element_type=jnp.float32) * inverse
    key_grad = jnp.dot(score_grad.T, q_head, preferred_element_type=jnp.float32) * inverse
    return (primal_low, tangent_low, query_grad.astype(jnp.bfloat16), key_grad.astype(jnp.bfloat16), value_grad.astype(jnp.bfloat16))

def reference(query_vectors, key_vectors, value_vectors, tangent_queries, tangent_keys, tangent_values, target_gap):
    stacked = tuple((heads_first(member) for member in (query_vectors, key_vectors, value_vectors, tangent_queries, tangent_keys, tangent_values, target_gap)))
    results = lax.map(one_head, stacked)
    return (heads_last(results[0]), heads_last(results[1]), heads_last(results[2]), heads_last(results[3]), heads_last(results[4]))
```

```python
import functools
import math

import jax
import jax.numpy as jnp
from jax import lax
from jax.experimental import pallas as pl
from jax.experimental.pallas import tpu as pltpu
from jax.sharding import PartitionSpec as P

HD = 128
MESH = pl.DeviceIdType.MESH

scale_loss = 64.0


def owner_of(head, nb):
    return (2 * head) % nb + (2 * head) // nb


def nt_dot(a, b):
    return lax.dot_general(a, b, (((1,), (1,)), ((), ())), preferred_element_type=jnp.float32)


def nn_dot(a, b):
    return jnp.dot(a, b, preferred_element_type=jnp.float32)


def kernel(nb, nh, hc, q_in, k_in, v_in, tq_in, tk_in, tv_in, g_in,
           po, to, dq, dk, dv,
           kk, qq, vv, gg, vt, kt, po_s, to_s, dq_s, dk_s, dv_s, dk_acc, dv_acc,
           in_send, in_recv, out_send, out_recv):
    b = lax.axis_index("blk")
    z = lax.axis_index("head")
    me = b * nh + z
    rows = q_in.shape[0]
    few = g_in.shape[0]
    seq = kk.shape[0]
    mine = b // 2 + (b % 2) * (nb // 2)
    is_owner = mine < hc
    inverse = 1.0 / math.sqrt(HD)
    log2e = 1.0 / math.log(2.0)

    barrier = pltpu.get_barrier_semaphore()

    def greet(p, carry):
        @pl.when(p != me)
        def _():
            pl.semaphore_signal(
                barrier, inc=1, device_id=(p // nh, p % nh), device_id_type=MESH
            )
        return carry

    lax.fori_loop(0, nb * nh, greet, 0)
    pl.semaphore_wait(barrier, nb * nh - 1)

    def send(src, dst, s_sem, r_sem, to_b, to_z):
        away = jnp.logical_or(to_b != b, to_z != z)

        @pl.when(away)
        def _():
            pltpu.make_async_remote_copy(
                src_ref=src, dst_ref=dst, send_sem=s_sem, recv_sem=r_sem,
                device_id=(to_b, to_z), device_id_type=MESH,
            ).start()

        @pl.when(jnp.logical_not(away))
        def _():
            pltpu.make_async_copy(src, dst, r_sem).start()

    def arrived(ref, sem):
        pltpu.make_async_copy(ref, ref, sem).wait()

    my_rows = pl.ds(pl.multiple_of(b * rows, rows), rows)
    inbound = (
        (k_in, kk, 0), (q_in, qq, 1), (tk_in, kk, 1), (tq_in, qq, 0),
        (v_in, vv, 0), (tv_in, vv, 1),
    )
    for at, (src, dst, half) in enumerate(inbound):
        for head in range(hc):
            send(
                src.at[:, pl.ds(head * HD, HD)],
                dst.at[my_rows, pl.ds(half * HD, HD)],
                in_send.at[at], in_recv.at[at], owner_of(head, nb), z,
            )
    few_rows = pl.ds(pl.multiple_of(me * few, few), few)
    for head in range(hc):
        def send_gap(plane, carry, head=head):
            columns = pl.ds(pl.multiple_of((plane * hc + head) * HD, HD), HD)
            send(
                g_in.at[:, columns], gg.at[few_rows, :],
                in_send.at[6], in_recv.at[6], owner_of(head, nb), plane,
            )
            return carry
        lax.fori_loop(0, nh, send_gap, 0)

    @pl.when(is_owner)
    def _():
        for at, (src, dst, half) in enumerate(inbound):
            arrived(dst.at[:, pl.ds(half * HD, HD)], in_recv.at[at])
        arrived(gg, in_recv.at[6])
        vt[...] = vv[...].T
        kt[...] = kk[:, :HD].T
        dk_acc[...] = jnp.zeros_like(dk_acc)
        dv_acc[...] = jnp.zeros_like(dv_acc)
        block = 256
        tiles = block // rows
        own_columns = pl.ds(pl.multiple_of(mine * HD, HD), HD)
        wide_columns = pl.ds(pl.multiple_of((z * hc + mine) * HD, HD), HD)

        def one_block(i, carry):
            at = pl.ds(pl.multiple_of(i * block, block), block)
            pair = qq[at, :]
            query = pair[:, HD:]
            s = nt_dot(kk[:, :HD], query)
            t = nt_dot(kk[...], pair)
            peak = jnp.max(s, axis=0, keepdims=True)
            w = jnp.exp2((s - peak) * (inverse * log2e))
            wt = w * t
            total = jnp.sum(w, axis=0, keepdims=True)
            tan_total = jnp.sum(wt, axis=0, keepdims=True)
            w_low = w.astype(jnp.bfloat16)
            t_low = wt.astype(jnp.bfloat16)
            sums = nn_dot(vt[...], w_low)
            more = nn_dot(vt[:HD, :], t_low)
            r = 1.0 / total
            primal = sums[:HD] * r
            tangent = (more * inverse + sums[HD:]) * r - (tan_total * inverse * r) * primal
            primal_low = primal.astype(jnp.bfloat16)
            tangent_low = tangent.astype(jnp.bfloat16)
            gap = gg[at, :].T.astype(jnp.float32)
            cot = (scale_loss * (gap + tangent_low.astype(jnp.float32))).astype(jnp.bfloat16)
            cot_r = (cot.astype(jnp.float32) * r).astype(jnp.bfloat16)
            inner = jnp.sum(
                cot_r.astype(jnp.float32) * primal_low.astype(jnp.float32), axis=0, keepdims=True
            )
            dp = nn_dot(vv[:, :HD], cot_r)
            ds = (w * (dp - inner)).astype(jnp.bfloat16)
            po_s[at, :] = primal_low.T
            to_s[at, :] = tangent_low.T
            dq_s[at, :] = (nn_dot(kt[...], ds) * inverse).astype(jnp.bfloat16).T
            dk_acc[...] += nn_dot(ds, query)
            dv_acc[...] += nn_dot(w_low, cot_r.T)
            for tile in range(tiles):
                to_b = i * tiles + tile
                start = pl.multiple_of(to_b * rows, rows)
                for plane in range(nh):
                    part = pl.ds(pl.multiple_of(start + plane * few, few), few)
                    send(po_s.at[part, :], po.at[:, wide_columns],
                         out_send.at[0], out_recv.at[0], to_b, plane)
                    send(to_s.at[part, :], to.at[:, wide_columns],
                         out_send.at[1], out_recv.at[1], to_b, plane)
                send(dq_s.at[pl.ds(start, rows), :], dq.at[:, own_columns],
                     out_send.at[2], out_recv.at[2], to_b, z)
            return carry

        lax.fori_loop(0, seq // block, one_block, 0)
        dk_s[...] = (dk_acc[...] * inverse).astype(jnp.bfloat16)
        dv_s[...] = dv_acc[...].astype(jnp.bfloat16)

        def send_grads(to_b, carry):
            part = pl.ds(pl.multiple_of(to_b * rows, rows), rows)
            send(dk_s.at[part, :], dk.at[:, own_columns],
                 out_send.at[3], out_recv.at[3], to_b, z)
            send(dv_s.at[part, :], dv.at[:, own_columns],
                 out_send.at[4], out_recv.at[4], to_b, z)
            return carry

        lax.fori_loop(0, nb, send_grads, 0)

    for at, ref in enumerate((po, to, dq, dk, dv)):
        arrived(ref, out_recv.at[at])

    @pl.when(is_owner)
    def _():
        for at, (src, dst, half) in enumerate(inbound):
            arrived(src.at[:, pl.ds(0, (hc - 1) * HD)], in_send.at[at])
        arrived(g_in.at[:, pl.ds(0, (nh * hc - 1) * HD)], in_send.at[6])
        for at, ref in enumerate((po_s, to_s)):
            arrived(ref.at[pl.ds(0, seq - few), :], out_send.at[at])
        for at, ref in enumerate((dq_s, dk_s, dv_s)):
            arrived(ref.at[pl.ds(0, seq - rows), :], out_send.at[at + 2])

    @pl.when(jnp.logical_not(is_owner))
    def _():
        for at, (src, dst, half) in enumerate(inbound):
            arrived(src, in_send.at[at])
        arrived(g_in, in_send.at[6])


def per_device(nb, nh, q, k, v, tq, tk, tv, g):
    rows, feat = q.shape
    hc = feat // HD
    seq = rows * nb
    low = jnp.bfloat16
    anywhere = pl.BlockSpec(memory_space=pl.ANY)
    wide = jax.ShapeDtypeStruct(g.shape, low)
    narrow = jax.ShapeDtypeStruct(q.shape, low)
    return pl.pallas_call(
        functools.partial(kernel, nb, nh, hc),
        out_shape=(wide, wide, narrow, narrow, narrow),
        in_specs=[anywhere] * 7,
        out_specs=(anywhere,) * 5,
        scratch_shapes=[
            pltpu.VMEM((seq, 2 * HD), low),
            pltpu.VMEM((seq, 2 * HD), low),
            pltpu.VMEM((seq, 2 * HD), low),
            pltpu.VMEM((seq, HD), low),
            pltpu.VMEM((2 * HD, seq), low),
            pltpu.VMEM((HD, seq), low),
            pltpu.VMEM((seq, HD), low),
            pltpu.VMEM((seq, HD), low),
            pltpu.VMEM((seq, HD), low),
            pltpu.VMEM((seq, HD), low),
            pltpu.VMEM((seq, HD), low),
            pltpu.VMEM((seq, HD), jnp.float32),
            pltpu.VMEM((seq, HD), jnp.float32),
            pltpu.SemaphoreType.DMA((7,)),
            pltpu.SemaphoreType.DMA((7,)),
            pltpu.SemaphoreType.DMA((5,)),
            pltpu.SemaphoreType.DMA((5,)),
        ],
        compiler_params=pltpu.CompilerParams(
            collective_id=0, has_side_effects=True, vmem_limit_bytes=58 * 2**20
        ),
    )(q, k, v, tq, tk, tv, g)


def solution(mesh):
    nb, nh = mesh.shape["blk"], mesh.shape["head"]
    narrow = P("blk", "head")
    wide = P(("blk", "head"), None)
    return jax.shard_map(
        functools.partial(per_device, nb, nh),
        mesh=mesh,
        in_specs=(narrow,) * 6 + (wide,),
        out_specs=(wide, wide, narrow, narrow, narrow),
        check_vma=False,
    )
```

```python
import functools
import math

import jax
import jax.numpy as jnp
from jax import lax
from jax.experimental import pallas as pl
from jax.experimental.pallas import tpu as pltpu
from jax.sharding import PartitionSpec as P

HD = 128
MESH = pl.DeviceIdType.MESH

scale_loss = 64.0


def nt_dot(a, b):
    return lax.dot_general(a, b, (((1,), (1,)), ((), ())), preferred_element_type=jnp.float32)


def nn_dot(a, b):
    return jnp.dot(a, b, preferred_element_type=jnp.float32)


def kernel(nb, nh, hc, q_in, k_in, v_in, tq_in, tk_in, tv_in, g_in,
           po, to, dq, dk, dv,
           kk, qq, vv, gg, vt, kt, po_s, to_s, dq_s, dk_s, dv_s, dk_acc, dv_acc,
           g_mid, po_mid, to_mid, dk_part, dv_part, dk_sum, dv_sum,
           in_send, in_recv, out_send, out_recv, mid_send, mid_recv, part_recv, sum_sem):
    b = lax.axis_index("blk")
    z = lax.axis_index("head")
    rows = q_in.shape[0]
    few = g_in.shape[0]
    seq = kk.shape[0]
    group = hc * HD
    block = 2 * rows
    last = hc - 1
    odd = b % 2
    helper = odd == 1
    owner = jnp.logical_and(odd == 0, b // 2 < last)
    idle = jnp.logical_and(odd == 0, b // 2 >= last)
    mine = (b // 2) * (1 - odd) + last * odd
    inverse = 1.0 / math.sqrt(HD)
    log2e = 1.0 / math.log(2.0)

    barrier = pltpu.get_barrier_semaphore()
    for step in range(1, nb):
        pl.semaphore_signal(
            barrier, inc=1, device_id=((b + step) % nb, z), device_id_type=MESH
        )
    for step in range(1, nh):
        pl.semaphore_signal(
            barrier, inc=1, device_id=(b, (z + step) % nh), device_id_type=MESH
        )
    pl.semaphore_wait(barrier, nb + nh - 2)

    def send(src, dst, s_sem, r_sem, to_b, to_z):
        away = jnp.logical_or(to_b != b, to_z != z)

        @pl.when(away)
        def _():
            pltpu.make_async_remote_copy(
                src_ref=src, dst_ref=dst, send_sem=s_sem, recv_sem=r_sem,
                device_id=(to_b, to_z), device_id_type=MESH,
            ).start()

        @pl.when(jnp.logical_not(away))
        def _():
            pltpu.make_async_copy(src, dst, r_sem).start()

    def arrived(ref, sem):
        pltpu.make_async_copy(ref, ref, sem).wait()

    def swap_planes(src_of, dst, at, s_sems, r_sems):
        for plane in range(nh):
            send(src_of(plane), dst, s_sems.at[at], r_sems.at[at], b, plane)

    my_rows = pl.ds(pl.multiple_of(b * rows, rows), rows)
    few_rows = pl.ds(pl.multiple_of(z * few, few), few)
    swap_planes(lambda plane: g_in.at[:, pl.ds(plane * group, group)],
                g_mid.at[few_rows, :], 2, mid_send, mid_recv)

    keys = ((k_in, kk, 0, 0), (tk_in, kk, 1, 2), (v_in, vv, 0, 4), (tv_in, vv, 1, 5))
    queries = ((q_in, qq, 1, 1), (tq_in, qq, 0, 3), (g_mid, gg, 0, 6))
    inbound = (keys[0], queries[0], keys[1], queries[1], keys[2], keys[3], queries[2])
    for member in inbound:
        src, dst, half, at = member
        if src is g_mid:
            arrived(g_mid, mid_recv.at[2])
        tail = src.at[:, pl.ds(last * HD, HD)]
        place = dst.at[my_rows, pl.ds(half * HD, HD)]
        for head in range(last):
            send(src.at[:, pl.ds(head * HD, HD)], place,
                 in_send.at[at], in_recv.at[at], 2 * head, z)
        if at in (0, 2, 4, 5):
            for step in range(nb // 2):
                send(tail, place, in_send.at[at], in_recv.at[at], 2 * step + 1, z)
        else:
            send(tail, place, in_send.at[at], in_recv.at[at], 2 * (b // 2) + 1, z)

    own_columns = pl.ds(pl.multiple_of(mine * HD, HD), HD)

    @pl.when(jnp.logical_not(idle))
    def _():
        for src, dst, half, at in keys:
            arrived(dst.at[:, pl.ds(half * HD, HD)], in_recv.at[at])
        for src, dst, half, at in queries:
            @pl.when(owner)
            def _():
                arrived(dst.at[:, pl.ds(half * HD, HD)], in_recv.at[at])

            @pl.when(helper)
            def _():
                arrived(
                    dst.at[pl.ds(pl.multiple_of((b // 2) * block, block), block),
                           pl.ds(half * HD, HD)],
                    in_recv.at[at],
                )
        vt[...] = vv[...].T
        kt[...] = kk[:, :HD].T
        dk_acc[...] = jnp.zeros_like(dk_acc)
        dv_acc[...] = jnp.zeros_like(dv_acc)

        def one_block(i, carry):
            at = pl.ds(pl.multiple_of(i * block, block), block)
            pair = qq[at, :]
            query = pair[:, HD:]
            s = nt_dot(kk[:, :HD], query)
            t = nt_dot(kk[...], pair)
            peak = jnp.max(s, axis=0, keepdims=True)
            w = jnp.exp2((s - peak) * (inverse * log2e))
            wt = w * t
            total = jnp.sum(w, axis=0, keepdims=True)
            tan_total = jnp.sum(wt, axis=0, keepdims=True)
            w_low = w.astype(jnp.bfloat16)
            t_low = wt.astype(jnp.bfloat16)
            sums = nn_dot(vt[...], w_low)
            more = nn_dot(vt[:HD, :], t_low)
            r = 1.0 / total
            primal = sums[:HD] * r
            tangent = (more * inverse + sums[HD:]) * r - (tan_total * inverse * r) * primal
            primal_low = primal.astype(jnp.bfloat16)
            tangent_low = tangent.astype(jnp.bfloat16)
            gap = gg[at, :].T.astype(jnp.float32)
            cot = (scale_loss * (gap + tangent_low.astype(jnp.float32))).astype(jnp.bfloat16)
            cot_r = (cot.astype(jnp.float32) * r).astype(jnp.bfloat16)
            inner = jnp.sum(
                cot_r.astype(jnp.float32) * primal_low.astype(jnp.float32), axis=0, keepdims=True
            )
            dp = nn_dot(vv[:, :HD], cot_r)
            ds = (w * (dp - inner)).astype(jnp.bfloat16)
            po_s[at, :] = primal_low.T
            to_s[at, :] = tangent_low.T
            dq_s[at, :] = (nn_dot(kt[...], ds) * inverse).astype(jnp.bfloat16).T
            dk_acc[...] += nn_dot(ds, query)
            dv_acc[...] += nn_dot(w_low, cot_r.T)
            for tile in range(2):
                to_b = 2 * i + tile
                part = pl.ds(pl.multiple_of(to_b * rows, rows), rows)
                send(po_s.at[part, :], po_mid.at[:, own_columns],
                     out_send.at[0], mid_recv.at[0], to_b, z)
                send(to_s.at[part, :], to_mid.at[:, own_columns],
                     out_send.at[1], mid_recv.at[1], to_b, z)
                send(dq_s.at[part, :], dq.at[:, own_columns],
                     out_send.at[2], out_recv.at[2], to_b, z)
            return carry

        first = odd * (b // 2)
        count = odd + (1 - odd) * (seq // block)
        lax.fori_loop(first, first + count, one_block, 0)
        dk_s[...] = (dk_acc[...] * inverse).astype(jnp.bfloat16)
        dv_s[...] = dv_acc[...].astype(jnp.bfloat16)

        @pl.when(owner)
        def _():
            for to_b in range(nb):
                part = pl.ds(to_b * rows, rows)
                send(dk_s.at[part, :], dk.at[:, own_columns],
                     out_send.at[3], out_recv.at[3], to_b, z)
                send(dv_s.at[part, :], dv.at[:, own_columns],
                     out_send.at[4], out_recv.at[4], to_b, z)

        @pl.when(helper)
        def _():
            slot = pl.ds(pl.multiple_of((b // 2) * rows, rows), rows)
            for to_b in range(nb):
                part = pl.ds(to_b * rows, rows)
                send(dk_s.at[part, :], dk_part.at[slot, :],
                     out_send.at[3], part_recv.at[0], to_b, z)
                send(dv_s.at[part, :], dv_part.at[slot, :],
                     out_send.at[4], part_recv.at[1], to_b, z)

    wide_columns = pl.ds(pl.multiple_of(z * group, group), group)
    for at, (mid, out) in enumerate(((po_mid, po), (to_mid, to))):
        arrived(mid, mid_recv.at[at])
        swap_planes(lambda plane: mid.at[pl.ds(plane * few, few), :],
                    out.at[:, wide_columns], at, mid_send, out_recv)
    sums = ((dk_part, dk_sum, dk), (dv_part, dv_sum, dv))
    for at, (part, result, out) in enumerate(sums):
        arrived(part, part_recv.at[at])
        held = part[pl.ds(0, rows), :].astype(jnp.float32)
        for step in range(1, nb // 2):
            held += part[pl.ds(step * rows, rows), :].astype(jnp.float32)
        result[...] = held.astype(jnp.bfloat16)
        pltpu.make_async_copy(result, out.at[:, pl.ds(last * HD, HD)], sum_sem.at[at]).start()

    for at, (part, result, out) in enumerate(sums):
        pltpu.make_async_copy(result, out.at[:, pl.ds(last * HD, HD)], sum_sem.at[at]).wait()
    for at, ref in enumerate((po, to, dq)):
        arrived(ref, out_recv.at[at])
    for at, ref in enumerate((dk, dv)):
        arrived(ref.at[:, pl.ds(0, last * HD)], out_recv.at[at + 3])

    for at in range(2):
        arrived(po_mid.at[pl.ds(0, (nh - 1) * few), :], mid_send.at[at])
    arrived(g_in.at[:, pl.ds(0, (nh - 1) * group)], mid_send.at[2])

    def tiles_left(count, sem):
        arrived(kk.at[pl.ds(0, count * rows), pl.ds(0, HD)], sem)

    for role, in_keys, in_queries in (
        (owner, last - 1 + nb // 2, last),
        (helper, last + nb // 2 - 1, last),
        (idle, last + nb // 2, hc),
    ):
        @pl.when(role)
        def _():
            for src, dst, half, at in keys:
                tiles_left(in_keys, in_send.at[at])
            for src, dst, half, at in queries:
                tiles_left(in_queries, in_send.at[at])
            if role is owner:
                for at in range(5):
                    tiles_left(nb - 1, out_send.at[at])
            if role is helper:
                for at in range(3):
                    tiles_left(1, out_send.at[at])
                for at in range(3, 5):
                    tiles_left(nb - 1, out_send.at[at])


def hand_over(*refs):
    sources, outs, held, sem = refs[:5], refs[5:10], refs[10:15], refs[15]
    loads = [pltpu.make_async_copy(sources[at], held[at], sem.at[0, at]) for at in range(5)]
    stores = [pltpu.make_async_copy(held[at], outs[at], sem.at[1, at]) for at in range(5)]
    for copy in loads:
        copy.start()
    for load, store in zip(loads, stores):
        load.wait()
        store.start()
    for copy in stores:
        copy.wait()


def per_device(nb, nh, q, k, v, tq, tk, tv, g):
    rows, feat = q.shape
    hc = feat // HD
    seq = rows * nb
    low = jnp.bfloat16
    anywhere = pl.BlockSpec(memory_space=pl.ANY)
    wide = jax.ShapeDtypeStruct(g.shape, low)
    narrow = jax.ShapeDtypeStruct(q.shape, low)
    shapes = (wide, wide, narrow, narrow, narrow)
    results = pl.pallas_call(
        functools.partial(kernel, nb, nh, hc),
        out_shape=shapes,
        in_specs=[anywhere] * 7,
        out_specs=(anywhere,) * 5,
        scratch_shapes=[
            pltpu.VMEM((seq, 2 * HD), low),
            pltpu.VMEM((seq, 2 * HD), low),
            pltpu.VMEM((seq, 2 * HD), low),
            pltpu.VMEM((seq, HD), low),
            pltpu.VMEM((2 * HD, seq), low),
            pltpu.VMEM((HD, seq), low),
            pltpu.VMEM((seq, HD), low),
            pltpu.VMEM((seq, HD), low),
            pltpu.VMEM((seq, HD), low),
            pltpu.VMEM((seq, HD), low),
            pltpu.VMEM((seq, HD), low),
            pltpu.VMEM((seq, HD), jnp.float32),
            pltpu.VMEM((seq, HD), jnp.float32),
            pltpu.VMEM((rows, feat), low),
            pltpu.VMEM((rows, feat), low),
            pltpu.VMEM((rows, feat), low),
            pltpu.VMEM((nb // 2 * rows, HD), low),
            pltpu.VMEM((nb // 2 * rows, HD), low),
            pltpu.VMEM((rows, HD), low),
            pltpu.VMEM((rows, HD), low),
            pltpu.SemaphoreType.DMA((7,)),
            pltpu.SemaphoreType.DMA((7,)),
            pltpu.SemaphoreType.DMA((5,)),
            pltpu.SemaphoreType.DMA((5,)),
            pltpu.SemaphoreType.DMA((3,)),
            pltpu.SemaphoreType.DMA((3,)),
            pltpu.SemaphoreType.DMA((2,)),
            pltpu.SemaphoreType.DMA((2,)),
        ],
        compiler_params=pltpu.CompilerParams(
            collective_id=0, has_side_effects=True, vmem_limit_bytes=58 * 2**20
        ),
    )(q, k, v, tq, tk, tv, g)
    return pl.pallas_call(
        hand_over,
        out_shape=shapes,
        in_specs=[anywhere] * 5,
        out_specs=(anywhere,) * 5,
        scratch_shapes=[pltpu.VMEM(shape.shape, low) for shape in shapes]
        + [pltpu.SemaphoreType.DMA((2, 5))],
    )(*results)


def solution(mesh):
    nb, nh = mesh.shape["blk"], mesh.shape["head"]
    narrow = P("blk", "head")
    wide = P(("blk", "head"), None)
    return jax.shard_map(
        functools.partial(per_device, nb, nh),
        mesh=mesh,
        in_specs=(narrow,) * 6 + (wide,),
        out_specs=(wide, wide, narrow, narrow, narrow),
        check_vma=False,
    )
```

```python
import functools
import math

import jax
import jax.numpy as jnp
from jax import lax
from jax.experimental import pallas as pl
from jax.experimental.pallas import tpu as pltpu
from jax.sharding import PartitionSpec as P

HD = 128
MESH = pl.DeviceIdType.MESH

scale_loss = 64.0


def nt_dot(a, b):
    return lax.dot_general(a, b, (((1,), (1,)), ((), ())), preferred_element_type=jnp.float32)


def nn_dot(a, b):
    return jnp.dot(a, b, preferred_element_type=jnp.float32)


def kernel(nb, nh, hc, q_in, k_in, v_in, tq_in, tk_in, tv_in, g_in,
           po, to, dq, dk, dv,
           kk, qq, vv, gg, vt, kt, po_s, to_s, dq_s, dk_s, dv_s, dk_acc, dv_acc,
           g_mid, po_mid, to_mid, dk_part, dv_part, dk_sum, dv_sum,
           in_send, in_recv, out_send, out_recv, mid_send, mid_recv, part_recv, sum_sem):
    b = lax.axis_index("blk")
    z = lax.axis_index("head")
    rows = q_in.shape[0]
    few = g_in.shape[0]
    seq = kk.shape[0]
    group = hc * HD
    block = 2 * rows
    last = hc - 1
    odd = b % 2
    helper = odd == 1
    owner = jnp.logical_and(odd == 0, b // 2 < last)
    idle = jnp.logical_and(odd == 0, b // 2 >= last)
    mine = (b // 2) * (1 - odd) + last * odd
    inverse = 1.0 / math.sqrt(HD)
    log2e = 1.0 / math.log(2.0)

    barrier = pltpu.get_barrier_semaphore()
    for step in range(1, nb):
        pl.semaphore_signal(
            barrier, inc=1, device_id=((b + step) % nb, z), device_id_type=MESH
        )
    for step in range(1, nh):
        pl.semaphore_signal(
            barrier, inc=1, device_id=(b, (z + step) % nh), device_id_type=MESH
        )
    pl.semaphore_wait(barrier, nb + nh - 2)

    def send(src, dst, s_sem, r_sem, to_b, to_z):
        away = jnp.logical_or(to_b != b, to_z != z)

        @pl.when(away)
        def _():
            pltpu.make_async_remote_copy(
                src_ref=src, dst_ref=dst, send_sem=s_sem, recv_sem=r_sem,
                device_id=(to_b, to_z), device_id_type=MESH,
            ).start()

        @pl.when(jnp.logical_not(away))
        def _():
            pltpu.make_async_copy(src, dst, r_sem).start()

    def arrived(ref, sem):
        pltpu.make_async_copy(ref, ref, sem).wait()

    def swap_planes(src_of, dst, at, s_sems, r_sems):
        for step in range(nh):
            plane = (z + 1 + step) % nh
            send(src_of(plane), dst, s_sems.at[at], r_sems.at[at], b, plane)

    my_rows = pl.ds(pl.multiple_of(b * rows, rows), rows)
    few_rows = pl.ds(pl.multiple_of(z * few, few), few)
    swap_planes(lambda plane: g_in.at[:, pl.ds(pl.multiple_of(plane * group, HD), group)],
                g_mid.at[few_rows, :], 2, mid_send, mid_recv)

    keys = ((k_in, kk, 0, 0), (tk_in, kk, 1, 2), (v_in, vv, 0, 4), (tv_in, vv, 1, 5))
    queries = ((q_in, qq, 1, 1), (tq_in, qq, 0, 3), (g_mid, gg, 0, 6))
    inbound = (keys[0], queries[0], keys[1], queries[1], keys[2], keys[3], queries[2])
    for member in inbound:
        src, dst, half, at = member
        if src is g_mid:
            arrived(g_mid, mid_recv.at[2])
        tail = src.at[:, pl.ds(last * HD, HD)]
        place = dst.at[my_rows, pl.ds(half * HD, HD)]
        for step in range(last):
            head = step
            send(src.at[:, pl.ds(pl.multiple_of(head * HD, HD), HD)], place,
                 in_send.at[at], in_recv.at[at], 2 * head, z)
        if at in (0, 2, 4, 5):
            for step in range(nb // 2):
                to_b = 2 * step + 1
                send(tail, place, in_send.at[at], in_recv.at[at], to_b, z)
        else:
            send(tail, place, in_send.at[at], in_recv.at[at], 2 * (b // 2) + 1, z)

    own_columns = pl.ds(pl.multiple_of(mine * HD, HD), HD)

    @pl.when(jnp.logical_not(idle))
    def _():
        for src, dst, half, at in keys[:2]:
            arrived(dst.at[:, pl.ds(half * HD, HD)], in_recv.at[at])

        def await_queries(member):
            src, dst, half, at = member

            @pl.when(owner)
            def _():
                arrived(dst.at[:, pl.ds(half * HD, HD)], in_recv.at[at])

            @pl.when(helper)
            def _():
                arrived(
                    dst.at[pl.ds(pl.multiple_of((b // 2) * block, block), block),
                           pl.ds(half * HD, HD)],
                    in_recv.at[at],
                )
        await_queries(queries[0])
        await_queries(queries[1])
        kt[...] = kk[:, :HD].T
        dk_acc[...] = jnp.zeros_like(dk_acc)
        dv_acc[...] = jnp.zeros_like(dv_acc)

        def one_block(turn, carry):
            i = (b // 2 + 1 - odd + turn) % (nb // 2)
            at = pl.ds(pl.multiple_of(i * block, block), block)
            pair = qq[at, :]
            query = pair[:, HD:]
            s = nt_dot(kk[:, :HD], query)
            t = nt_dot(kk[...], pair)
            peak = jnp.max(s, axis=0, keepdims=True)
            w = jnp.exp2((s - peak) * (inverse * log2e))
            wt = w * t
            total = jnp.sum(w, axis=0, keepdims=True)
            tan_total = jnp.sum(wt, axis=0, keepdims=True)
            w_low = w.astype(jnp.bfloat16)
            t_low = wt.astype(jnp.bfloat16)

            @pl.when(turn == 0)
            def _():
                for src, dst, half, at in keys[2:]:
                    arrived(dst.at[:, pl.ds(half * HD, HD)], in_recv.at[at])
                await_queries(queries[2])
                vt[...] = vv[...].T

            sums = nn_dot(vt[...], w_low)
            more = nn_dot(vt[:HD, :], t_low)
            r = 1.0 / total
            primal = sums[:HD] * r
            tangent = (more * inverse + sums[HD:]) * r - (tan_total * inverse * r) * primal
            primal_low = primal.astype(jnp.bfloat16)
            tangent_low = tangent.astype(jnp.bfloat16)
            gap = gg[at, :].T.astype(jnp.float32)
            cot = (scale_loss * (gap + tangent_low.astype(jnp.float32))).astype(jnp.bfloat16)
            cot_r = (cot.astype(jnp.float32) * r).astype(jnp.bfloat16)
            inner = jnp.sum(
                cot_r.astype(jnp.float32) * primal_low.astype(jnp.float32), axis=0, keepdims=True
            )
            dp = nn_dot(vv[:, :HD], cot_r)
            ds = (w * (dp - inner)).astype(jnp.bfloat16)
            po_s[at, :] = primal_low.T
            to_s[at, :] = tangent_low.T
            dq_s[at, :] = (nn_dot(kt[...], ds) * inverse).astype(jnp.bfloat16).T
            dk_acc[...] += nn_dot(ds, query)
            dv_acc[...] += nn_dot(w_low, cot_r.T)
            for tile in range(2):
                to_b = 2 * i + tile
                part = pl.ds(pl.multiple_of(to_b * rows, rows), rows)
                send(po_s.at[part, :], po_mid.at[:, own_columns],
                     out_send.at[0], mid_recv.at[0], to_b, z)
                send(to_s.at[part, :], to_mid.at[:, own_columns],
                     out_send.at[1], mid_recv.at[1], to_b, z)
                send(dq_s.at[part, :], dq.at[:, own_columns],
                     out_send.at[2], out_recv.at[2], to_b, z)
            return carry

        count = odd + (1 - odd) * (seq // block)
        lax.fori_loop(0, count, one_block, 0)
        dk_s[...] = (dk_acc[...] * inverse).astype(jnp.bfloat16)
        dv_s[...] = dv_acc[...].astype(jnp.bfloat16)

        @pl.when(owner)
        def _():
            for step in range(nb):
                to_b = step
                part = pl.ds(pl.multiple_of(to_b * rows, rows), rows)
                send(dk_s.at[part, :], dk.at[:, own_columns],
                     out_send.at[3], out_recv.at[3], to_b, z)
                send(dv_s.at[part, :], dv.at[:, own_columns],
                     out_send.at[4], out_recv.at[4], to_b, z)

        @pl.when(helper)
        def _():
            slot = pl.ds(pl.multiple_of((b // 2) * rows, rows), rows)
            for step in range(nb):
                to_b = step
                part = pl.ds(pl.multiple_of(to_b * rows, rows), rows)
                send(dk_s.at[part, :], dk_part.at[slot, :],
                     out_send.at[3], part_recv.at[0], to_b, z)
                send(dv_s.at[part, :], dv_part.at[slot, :],
                     out_send.at[4], part_recv.at[1], to_b, z)

    wide_columns = pl.ds(pl.multiple_of(z * group, group), group)
    for at, (mid, out) in enumerate(((po_mid, po), (to_mid, to))):
        arrived(mid, mid_recv.at[at])
        swap_planes(lambda plane: mid.at[pl.ds(pl.multiple_of(plane * few, few), few), :],
                    out.at[:, wide_columns], at, mid_send, out_recv)
    sums = ((dk_part, dk_sum, dk), (dv_part, dv_sum, dv))
    for at, (part, result, out) in enumerate(sums):
        arrived(part, part_recv.at[at])
        held = part[pl.ds(0, rows), :].astype(jnp.float32)
        for step in range(1, nb // 2):
            held += part[pl.ds(step * rows, rows), :].astype(jnp.float32)
        result[...] = held.astype(jnp.bfloat16)
        pltpu.make_async_copy(result, out.at[:, pl.ds(last * HD, HD)], sum_sem.at[at]).start()

    for at, (part, result, out) in enumerate(sums):
        pltpu.make_async_copy(result, out.at[:, pl.ds(last * HD, HD)], sum_sem.at[at]).wait()
    for at, ref in enumerate((po, to, dq)):
        arrived(ref, out_recv.at[at])
    for at, ref in enumerate((dk, dv)):
        arrived(ref.at[:, pl.ds(0, last * HD)], out_recv.at[at + 3])

    for at in range(2):
        arrived(po_mid.at[pl.ds(0, (nh - 1) * few), :], mid_send.at[at])
    arrived(g_in.at[:, pl.ds(0, (nh - 1) * group)], mid_send.at[2])

    def tiles_left(count, sem):
        arrived(kk.at[pl.ds(0, count * rows), pl.ds(0, HD)], sem)

    for role, in_keys, in_queries in (
        (owner, last - 1 + nb // 2, last),
        (helper, last + nb // 2 - 1, last),
        (idle, last + nb // 2, hc),
    ):
        @pl.when(role)
        def _():
            for src, dst, half, at in keys:
                tiles_left(in_keys, in_send.at[at])
            for src, dst, half, at in queries:
                tiles_left(in_queries, in_send.at[at])
            if role is owner:
                for at in range(5):
                    tiles_left(nb - 1, out_send.at[at])
            if role is helper:
                for at in range(3):
                    tiles_left(1, out_send.at[at])
                for at in range(3, 5):
                    tiles_left(nb - 1, out_send.at[at])


def hand_over(*refs):
    sources, outs, held, sem = refs[:5], refs[5:10], refs[10:15], refs[15]
    loads = [pltpu.make_async_copy(sources[at], held[at], sem.at[0, at]) for at in range(5)]
    stores = [pltpu.make_async_copy(held[at], outs[at], sem.at[1, at]) for at in range(5)]
    for copy in loads:
        copy.start()
    for load, store in zip(loads, stores):
        load.wait()
        store.start()
    for copy in stores:
        copy.wait()


def per_device(nb, nh, q, k, v, tq, tk, tv, g):
    rows, feat = q.shape
    hc = feat // HD
    seq = rows * nb
    low = jnp.bfloat16
    anywhere = pl.BlockSpec(memory_space=pl.ANY)
    wide = jax.ShapeDtypeStruct(g.shape, low)
    narrow = jax.ShapeDtypeStruct(q.shape, low)
    shapes = (wide, wide, narrow, narrow, narrow)
    results = pl.pallas_call(
        functools.partial(kernel, nb, nh, hc),
        out_shape=shapes,
        in_specs=[anywhere] * 7,
        out_specs=(anywhere,) * 5,
        scratch_shapes=[
            pltpu.VMEM((seq, 2 * HD), low),
            pltpu.VMEM((seq, 2 * HD), low),
            pltpu.VMEM((seq, 2 * HD), low),
            pltpu.VMEM((seq, HD), low),
            pltpu.VMEM((2 * HD, seq), low),
            pltpu.VMEM((HD, seq), low),
            pltpu.VMEM((seq, HD), low),
            pltpu.VMEM((seq, HD), low),
            pltpu.VMEM((seq, HD), low),
            pltpu.VMEM((seq, HD), low),
            pltpu.VMEM((seq, HD), low),
            pltpu.VMEM((seq, HD), jnp.float32),
            pltpu.VMEM((seq, HD), jnp.float32),
            pltpu.VMEM((rows, feat), low),
            pltpu.VMEM((rows, feat), low),
            pltpu.VMEM((rows, feat), low),
            pltpu.VMEM((nb // 2 * rows, HD), low),
            pltpu.VMEM((nb // 2 * rows, HD), low),
            pltpu.VMEM((rows, HD), low),
            pltpu.VMEM((rows, HD), low),
            pltpu.SemaphoreType.DMA((7,)),
            pltpu.SemaphoreType.DMA((7,)),
            pltpu.SemaphoreType.DMA((5,)),
            pltpu.SemaphoreType.DMA((5,)),
            pltpu.SemaphoreType.DMA((3,)),
            pltpu.SemaphoreType.DMA((3,)),
            pltpu.SemaphoreType.DMA((2,)),
            pltpu.SemaphoreType.DMA((2,)),
        ],
        compiler_params=pltpu.CompilerParams(
            collective_id=0, has_side_effects=True, vmem_limit_bytes=58 * 2**20
        ),
    )(q, k, v, tq, tk, tv, g)
    return pl.pallas_call(
        hand_over,
        out_shape=shapes,
        in_specs=[anywhere] * 5,
        out_specs=(anywhere,) * 5,
        scratch_shapes=[pltpu.VMEM(shape.shape, low) for shape in shapes]
        + [pltpu.SemaphoreType.DMA((2, 5))],
    )(*results)


def solution(mesh):
    nb, nh = mesh.shape["blk"], mesh.shape["head"]
    narrow = P("blk", "head")
    wide = P(("blk", "head"), None)
    return jax.shard_map(
        functools.partial(per_device, nb, nh),
        mesh=mesh,
        in_specs=(narrow,) * 6 + (wide,),
        out_specs=(wide, wide, narrow, narrow, narrow),
        check_vma=False,
    )
```
